32 devices in a mesh: wide: 8 (over z, y), rep: 4 (over x, core).
Axes of the slice: x: 2, y: 2, z: 4, core: 2. Of those that a mesh axis runs over, the one named last changes fastest.
Arguments:
- integrals: float32 [8, 1, 512, 512], P('wide', None, 'rep'), may hold values from -0.25 to 0.25
- driver: float32 [8, 256, 1, 512], P(None, 'wide', None, 'rep'), may hold values from -12 to 12
- occ_energy: float32 [8, 256], P(None, 'wide'), may hold values from -2 to -0.5
- vir_energy: float32 [8, 1, 512], P(None, None, 'rep'), may hold values from 1 to 8
- occ_count: int32 [8], replicated, may hold values from 64 to 256, as said below
- tile_width: int32 [8, 1], replicated, may hold values from 128 to 512, as said below
Outputs:
- amplitudes: float32 [8, 256, 1, 512], P(None, 'wide', None, 'rep')
The draws below stay inside these ranges and needn't reach their ends.
Inputs may be any that keep to these rules, and one draw needn't show every extreme that they name: `occ_count`: some pair irrep has all 256 rows live and some has 64. `tile_width`: some tile is fully live and some has 128 live pairs.
All inputs are finite; a program needn't handle non-finite values.
Results may differ from the reference program's by a relative error of at most 0.0001.
Values sent between devices are 32-bit elements; how exact they have to be, the bound alone decides.
A program may use at most 128 MiB of HBM per device.

```python
import math
import jax
import jax.numpy as jnp
from jax import lax

NIRREP = 8
OT = 256
TW = 512
ITERS = 2
NTL = 1
N_WIDE = 8


def draw_occ_count(key, part):
    key = jax.random.fold_in(key, 11)
    key_values, key_order = jax.random.split(key)
    counts = jax.random.randint(key_values, (NIRREP,), OT // 4, OT + 1)
    ranking = jax.random.permutation(key_order, NIRREP)
    counts = counts.at[ranking[0]].set(OT)
    counts = counts.at[ranking[1]].set(OT // 4)
    return counts.astype(jnp.int32)


def draw_tile_width(key, part):
    key = jax.random.fold_in(key, 23)
    key_values, key_order = jax.random.split(key)
    widths = jax.random.randint(key_values, (NIRREP * NTL,), TW // 4, TW + 1)
    ranking = jax.random.permutation(key_order, NIRREP * NTL)
    widths = widths.at[ranking[0]].set(TW)
    widths = widths.at[ranking[1]].set(TW // 4)
    return widths.reshape(NIRREP, NTL).astype(jnp.int32)


def steps_of(rng, dims, pieces, smallest, top_value):
    def one(axis_at, blocks):
        steps = jax.random.uniform(jax.random.fold_in(jax.random.fold_in(rng, 6), axis_at), (blocks,), jnp.float32, smallest / len(pieces), top_value / len(pieces))
        return jnp.repeat(jnp.exp(steps), dims[axis_at] // blocks).reshape((-1,) + (1,) * (len(dims) - axis_at - 1))

    gain = one(*pieces[0])
    for cut in pieces[1:]:
        gain = gain * one(*cut)
    return gain


def normal_values(own_key, shape, scale, reach, shards=(), held_as=jnp.bfloat16):
    gain = steps_of(own_key, shape, shards, -0.22, 0.18) if shards else 1.0
    result = jax.random.normal(own_key, shape, jnp.float32) * scale * gain
    return jnp.minimum(jnp.maximum(result, -reach), reach).astype(held_as)


def setup_inputs(seed: int = 0) -> dict:
    keys = jax.random.split(jax.random.key(seed), 7)
    integrals = normal_values(keys[0], (N_WIDE, NTL, TW, TW), (NTL * TW) ** -0.5, 0.25, ((0, 8), (2, 4)), jnp.float32)
    driver = normal_values(keys[1], (NIRREP, OT, NTL, TW), 2.0, 12.0, ((1, 8), (3, 4)), jnp.float32)
    occ_energy = jnp.clip(-2.0 + 1.5 * jax.random.uniform(keys[2], (NIRREP, OT), jnp.float32) ** steps_of(keys[2], (NIRREP, OT), ((1, 8),), -0.2, 0.2), -2.0, -0.5)
    vir_energy = jnp.clip(jnp.exp(math.log(8.0) - 2.0794415 * jax.random.uniform(keys[3], (NIRREP, NTL, TW), jnp.float32) ** steps_of(keys[3], (NIRREP, NTL, TW), ((2, 4),), -0.2, 0.2)), 1.0, 8.0)
    occ_count = draw_occ_count(jax.random.fold_in(keys[6], 71), 0)
    tile_width = draw_tile_width(jax.random.fold_in(keys[6], 71), 0)
    return {"integrals": integrals, "driver": driver, "occ_energy": occ_energy, "vir_energy": vir_energy, "occ_count": occ_count, "tile_width": tile_width}


def reference(integrals, driver, occ_energy, vir_energy, occ_count, tile_width):
    rows_live = jnp.arange(OT, dtype=jnp.int32)[None, :] < occ_count[:, None]
    cols_live = jnp.arange(TW, dtype=jnp.int32)[None, None, :] < tile_width[:, :, None]
    live_mask = (rows_live[:, :, None, None] & cols_live[:, None, :, :]).astype(jnp.float32)
    weighting = live_mask / (vir_energy[:, None, :, :] - occ_energy[:, :, None, None])
    amplitudes = driver * weighting
    blocks = integrals.reshape(NIRREP, NTL, NTL, TW, TW)

    def ladder_block(pair):
        tile_amps, tile_ints = pair
        return jnp.einsum("ojc,kjcd->okd", tile_amps, tile_ints, precision=lax.Precision.HIGHEST)

    for sweep in range(ITERS):
        ladder = lax.map(ladder_block, (amplitudes, blocks))
        amplitudes = (driver + ladder) * weighting
    return amplitudes
```

```python
import functools

import jax
import jax.numpy as jnp
from jax import lax
from jax.experimental import pallas as pl
from jax.experimental.pallas import tpu as pltpu
from jax.sharding import PartitionSpec as P

ITERS = 2
MESH = pl.DeviceIdType.MESH
F32 = jnp.float32
BF16 = jnp.bfloat16


def split(value):
    high = value.astype(BF16)
    low = (value - high.astype(F32)).astype(BF16)
    return high, low


def product(high, low, weight_high, weight_low):
    dot = functools.partial(jnp.dot, preferred_element_type=F32)
    return dot(high, weight_high) + (dot(low, weight_high) + dot(high, weight_low))


def ladder_kernel(
    n_wide, n_rep, chunks,
    count_ref, width_ref, v_ref, d_ref, occ_ref, vir_ref, out_ref,
    v_all, v_high, v_low, d_all, a_high, a_low, e_src, e_all, vir_src, vir_all, stage,
    chip_send, chip_recv, pair_send, pair_recv, relay_send, relay_recv,
    d_send, d_recv, e_send, e_recv, vir_send, vir_recv, out_send, out_recv,
):
    wide = lax.axis_index("wide")
    rep = lax.axis_index("rep")
    total = n_wide * n_rep
    me = wide * n_rep + rep
    depth, width = v_ref.shape
    sub = 8
    row_count = sub * n_rep
    rows = n_wide * sub
    half = lax.div(rep, 2)
    pair = rep + 1 - 2 * lax.rem(rep, 2)
    mirror = lax.rem(rep + 2, n_rep)
    piece = depth // chunks

    barrier = pltpu.get_barrier_semaphore()

    def greet(step, carry):
        other = lax.rem(me + step, total)
        pl.semaphore_signal(
            barrier, inc=1, device_id=(lax.div(other, n_rep), lax.rem(other, n_rep)), device_id_type=MESH
        )
        return carry

    lax.fori_loop(1, total, greet, 0)

    lane = lax.broadcasted_iota(jnp.int32, (sub, row_count), 1)
    sublane = lax.broadcasted_iota(jnp.int32, (sub, row_count), 0)
    pick = lane == sublane + rep * sub
    for group in range(n_wide):
        row = jnp.broadcast_to(occ_ref[group:group + 1, :], (sub, row_count))
        column = jnp.sum(jnp.where(pick, row, 0.0), axis=1, keepdims=True)
        e_src[group] = jnp.broadcast_to(column, (sub, 128))
    vir_src[...] = jnp.broadcast_to(vir_ref[pl.ds(wide, 1), :], vir_src.shape)

    pl.semaphore_wait(barrier, total - 1)

    chip_copies = []
    for chunk in range(chunks):
        span = pl.ds(chunk * piece, piece)
        copy = pltpu.make_async_remote_copy(
            src_ref=v_ref.at[span], dst_ref=v_all.at[rep, span],
            send_sem=chip_send.at[chunk], recv_sem=chip_recv.at[chunk],
            device_id=(wide, mirror), device_id_type=MESH,
        )
        copy.start()
        chip_copies.append(copy)
    pair_copy = pltpu.make_async_remote_copy(
        src_ref=v_ref, dst_ref=v_all.at[rep], send_sem=pair_send, recv_sem=pair_recv,
        device_id=(wide, pair), device_id_type=MESH,
    )
    pair_copy.start()

    def send_driver(step, carry):
        other = lax.rem(me + step, total)
        group = lax.div(other, n_rep)
        share = lax.rem(other, n_rep)
        pltpu.make_async_remote_copy(
            src_ref=d_ref.at[pl.ds(pl.multiple_of(group * row_count + share * sub, sub), sub)],
            dst_ref=d_all.at[rep, pl.ds(pl.multiple_of(wide * sub, sub), sub)],
            send_sem=d_send, recv_sem=d_recv,
            device_id=(group, share), device_id_type=MESH,
        ).start()
        return carry

    lax.fori_loop(1, total, send_driver, 0)
    pltpu.make_async_copy(
        d_ref.at[pl.ds(pl.multiple_of(wide * row_count + rep * sub, sub), sub)],
        d_all.at[rep, pl.ds(pl.multiple_of(wide * sub, sub), sub)],
        d_recv,
    ).start()
    for step in range(1, n_rep):
        pltpu.make_async_remote_copy(
            src_ref=vir_src, dst_ref=vir_all.at[rep], send_sem=vir_send, recv_sem=vir_recv,
            device_id=(wide, lax.rem(rep + step, n_rep)), device_id_type=MESH,
        ).start()
    pltpu.make_async_copy(vir_src, vir_all.at[rep], vir_recv).start()
    for step in range(1, n_wide):
        group = lax.rem(wide + step, n_wide)
        pltpu.make_async_remote_copy(
            src_ref=e_src.at[group], dst_ref=e_all.at[wide], send_sem=e_send, recv_sem=e_recv,
            device_id=(group, rep), device_id_type=MESH,
        ).start()
    pltpu.make_async_copy(e_src.at[wide], e_all.at[wide], e_recv).start()

    def hold(block, value):
        high, low = split(value)
        v_high[block] = high
        v_low[block] = low

    hold(rep, v_ref[...])
    pair_copy.wait_recv()
    hold(pair, v_all[pair])

    pltpu.make_async_copy(e_all, e_all, e_recv).wait()
    pltpu.make_async_copy(vir_all, vir_all, vir_recv).wait()
    pltpu.make_async_copy(d_all, d_all, d_recv).wait()

    count = count_ref[wide]
    live_width = width_ref[wide]
    local = lax.broadcasted_iota(jnp.int32, (rows, 128), 0)
    row_id = lax.div(local, sub) * row_count + rep * sub + lax.rem(local, sub)
    col_id = lax.broadcasted_iota(jnp.int32, (rows, 128), 1)
    occ = e_all[...].reshape(rows, 128)
    weighting = []
    for block in range(n_rep):
        live = ((row_id < count) & (col_id + block * depth < live_width)).astype(F32)
        vir = jnp.broadcast_to(vir_all[block, 0:1, :], (rows, 128))
        weighting.append(live / (vir - occ))
    driver = [d_all[block] for block in range(n_rep)]
    for block in range(n_rep):
        high, low = split(driver[block] * weighting[block])
        a_high[block] = high
        a_low[block] = low

    def half_product(which):
        first = 2 * which
        return product(
            jnp.concatenate([a_high[first], a_high[first + 1]], axis=1),
            jnp.concatenate([a_low[first], a_low[first + 1]], axis=1),
            v_high[pl.ds(first, 2)].reshape(2 * depth, width),
            v_low[pl.ds(first, 2)].reshape(2 * depth, width),
        )

    ladder = half_product(half)

    relays = []
    for chunk in range(chunks):
        span = pl.ds(chunk * piece, piece)
        chip_copies[chunk].wait_recv()
        relay = pltpu.make_async_remote_copy(
            src_ref=v_all.at[mirror, span], dst_ref=v_all.at[mirror, span],
            send_sem=relay_send.at[chunk], recv_sem=relay_recv.at[chunk],
            device_id=(wide, pair), device_id_type=MESH,
        )
        relay.start()
        relays.append(relay)
    hold(mirror, v_all[mirror])
    for relay in relays:
        relay.wait_recv()
    far = lax.rem(pair + 2, n_rep)
    hold(far, v_all[far])
    ladder = ladder + half_product(1 - half)

    for sweep in range(1, ITERS):
        for block in range(n_rep):
            part = ladder[:, block * depth:(block + 1) * depth]
            high, low = split((driver[block] + part) * weighting[block])
            a_high[block] = high
            a_low[block] = low
        ladder = half_product(0) + half_product(1)
    for block in range(n_rep):
        part = ladder[:, block * depth:(block + 1) * depth]
        stage[block] = (driver[block] + part) * weighting[block]

    def send_out(step, carry):
        other = lax.rem(me + step, total)
        owner = lax.div(other, n_rep)
        block = lax.rem(other, n_rep)
        pltpu.make_async_remote_copy(
            src_ref=stage.at[block, pl.ds(pl.multiple_of(owner * sub, sub), sub)],
            dst_ref=out_ref.at[pl.ds(pl.multiple_of(wide * row_count + rep * sub, sub), sub)],
            send_sem=out_send, recv_sem=out_recv,
            device_id=(owner, block), device_id_type=MESH,
        ).start()
        return carry

    lax.fori_loop(1, total, send_out, 0)
    pltpu.make_async_copy(
        stage.at[rep, pl.ds(pl.multiple_of(wide * sub, sub), sub)],
        out_ref.at[pl.ds(pl.multiple_of(wide * row_count + rep * sub, sub), sub)],
        out_recv,
    ).start()

    for copy in chip_copies:
        copy.wait_send()
    pair_copy.wait_send()
    for relay in relays:
        relay.wait_send()
    sent = d_ref.at[pl.ds(0, (total - 1) * sub)]
    pltpu.make_async_copy(sent, sent, d_send).wait()
    sent = e_src.at[pl.ds(0, n_wide - 1)]
    pltpu.make_async_copy(sent, sent, e_send).wait()
    sent = vir_all.at[pl.ds(0, n_rep - 1)]
    pltpu.make_async_copy(sent, sent, vir_send).wait()
    sent = d_ref.at[pl.ds(0, (total - 1) * sub)]
    pltpu.make_async_copy(sent, sent, out_send).wait()
    pltpu.make_async_copy(out_ref, out_ref, out_recv).wait()


def group_shards(integrals, driver, occ_energy, vir_energy, occ_count, tile_width):
    n_wide = lax.axis_size("wide")
    n_rep = lax.axis_size("rep")
    groups, row_count, _, depth = driver.shape
    width = integrals.shape[3]
    sub = row_count // n_rep
    rows = n_wide * sub
    chunks = 4
    vmem = pl.BlockSpec(memory_space=pltpu.VMEM)
    smem = pl.BlockSpec(memory_space=pltpu.SMEM)
    dma = pltpu.SemaphoreType.DMA
    out = pl.pallas_call(
        functools.partial(ladder_kernel, n_wide, n_rep, chunks),
        out_shape=jax.ShapeDtypeStruct((groups * row_count, depth), F32),
        in_specs=[smem, smem, vmem, vmem, vmem, vmem],
        out_specs=vmem,
        scratch_shapes=[
            pltpu.VMEM((n_rep, depth, width), F32),
            pltpu.VMEM((n_rep, depth, width), BF16),
            pltpu.VMEM((n_rep, depth, width), BF16),
            pltpu.VMEM((n_rep, rows, depth), F32),
            pltpu.VMEM((n_rep, rows, depth), BF16),
            pltpu.VMEM((n_rep, rows, depth), BF16),
            pltpu.VMEM((n_wide, sub, 128), F32),
            pltpu.VMEM((n_wide, sub, 128), F32),
            pltpu.VMEM((8, 128), F32),
            pltpu.VMEM((n_rep, 8, 128), F32),
            pltpu.VMEM((n_rep, rows, depth), F32),
            dma((chunks,)), dma((chunks,)), dma, dma, dma((chunks,)), dma((chunks,)),
            dma, dma, dma, dma, dma, dma, dma, dma,
        ],
        compiler_params=pltpu.CompilerParams(
            collective_id=0, has_side_effects=True, vmem_limit_bytes=32 * 1024 * 1024
        ),
        name="ladder_sweeps",
    )(
        occ_count,
        tile_width.reshape(groups),
        integrals.reshape(depth, width),
        driver.reshape(groups * row_count, depth),
        occ_energy,
        vir_energy.reshape(groups, depth),
    )
    return out.reshape(groups, row_count, 1, depth)


def tiled_shards(integrals, driver, occ_energy, vir_energy, occ_count, tile_width):
    n_wide = lax.axis_size("wide")
    wide_index = lax.axis_index("wide")
    rep_index = lax.axis_index("rep")
    groups = driver.shape[0]
    row_count = driver.shape[1]
    tile_count = driver.shape[2]
    quarter = driver.shape[3]
    out_width = integrals.shape[3]
    all_rows = row_count * n_wide
    row_ids = wide_index * row_count + jnp.arange(row_count, dtype=jnp.int32)
    col_ids = rep_index * quarter + jnp.arange(quarter, dtype=jnp.int32)
    rows_live = row_ids[None, :] < occ_count[:, None]
    cols_live = col_ids[None, None, :] < tile_width[:, :, None]
    live_mask = (rows_live[:, :, None, None] & cols_live[:, None, :, :]).astype(jnp.float32)
    weighting = live_mask / (vir_energy[:, None, :, :] - occ_energy[:, :, None, None])
    amplitudes = driver * weighting
    weights = integrals.reshape(tile_count * quarter, out_width)
    for sweep in range(ITERS):

        def add_tile(tile_index, running):
            tile_piece = lax.dynamic_index_in_dim(amplitudes, tile_index, 2, keepdims=False)
            outgoing = jnp.broadcast_to(
                tile_piece[:, None], (groups, n_wide // groups, row_count, quarter)
            )
            outgoing = outgoing.reshape(n_wide, row_count, quarter)
            received = lax.all_to_all(outgoing, "wide", split_axis=0, concat_axis=1, tiled=True)
            tile_rows = received.reshape(all_rows, quarter)
            tile_slice = lax.dynamic_slice_in_dim(weights, tile_index * quarter, quarter, 0)
            return running + jnp.dot(
                tile_rows,
                tile_slice,
                precision=lax.Precision.HIGHEST,
                preferred_element_type=jnp.float32,
            )

        partial_value = lax.fori_loop(
            0, tile_count, add_tile, jnp.zeros((all_rows, out_width), jnp.float32)
        )
        reduced = lax.psum_scatter(partial_value, "rep", scatter_dimension=1, tiled=True)
        returned = lax.all_to_all(
            reduced.reshape(1, all_rows, quarter),
            "wide",
            split_axis=1,
            concat_axis=0,
            tiled=True,
        )
        returned = returned.reshape(groups, tile_count, row_count, quarter)
        amplitudes = (driver + jnp.transpose(returned, (0, 2, 1, 3))) * weighting
    return amplitudes


def shards(integrals, driver, occ_energy, vir_energy, occ_count, tile_width):
    n_wide = lax.axis_size("wide")
    n_rep = lax.axis_size("rep")
    groups, row_count, tile_count, depth = driver.shape
    fits = tile_count == 1 and groups == n_wide and n_rep == 4 and row_count == 8 * n_rep and depth == 128
    body = group_shards if fits else tiled_shards
    return body(integrals, driver, occ_energy, vir_energy, occ_count, tile_width)


def solution(mesh):
    placed = (
        P("wide", None, "rep", None),
        P(None, "wide", None, "rep"),
        P(None, "wide"),
        P(None, None, "rep"),
        P(),
        P(),
    )
    return jax.shard_map(
        shards, mesh=mesh, in_specs=placed, out_specs=P(None, "wide", None, "rep"), check_vma=False
    )
```

```python
import functools

import jax
import jax.numpy as jnp
from jax import lax
from jax.experimental import pallas as pl
from jax.experimental.pallas import tpu as pltpu
from jax.sharding import PartitionSpec as P

ITERS = 2
MESH = pl.DeviceIdType.MESH
F32 = jnp.float32
BF16 = jnp.bfloat16


def split(value):
    high = value.astype(BF16)
    low = (value - high.astype(F32)).astype(BF16)
    return high, low


def product(high, low, weight_high, weight_low):
    dot = functools.partial(jnp.dot, preferred_element_type=F32)
    return dot(high, weight_high) + (dot(low, weight_high) + dot(high, weight_low))


def ladder_kernel(
    n_wide, n_rep, chunks,
    count_in, width_in, v_ref, d_ref, occ_in, vir_in, out_ref,
    count_ref, width_ref, occ_ref, vir_ref, load_sem, v_load, v_all, v_high, v_low, d_all, a_high, a_low, e_src, e_all, vir_src, vir_all, stage,
    chip_send, chip_recv, pair_send, pair_recv, relay_send, relay_recv,
    d_send, d_recv, e_send, e_recv, vir_send, vir_recv, out_send, out_recv,
):
    wide = lax.axis_index("wide")
    rep = lax.axis_index("rep")
    total = n_wide * n_rep
    me = wide * n_rep + rep
    depth, width = v_ref.shape
    sub = 8
    row_count = sub * n_rep
    rows = n_wide * sub
    half = lax.div(rep, 2)
    pair = rep + 1 - 2 * lax.rem(rep, 2)
    mirror = lax.rem(rep + 2, n_rep)
    piece = depth // chunks

    barrier = pltpu.get_barrier_semaphore()

    def greet(step, carry):
        other = lax.rem(me + step, total)
        pl.semaphore_signal(
            barrier, inc=1, device_id=(lax.div(other, n_rep), lax.rem(other, n_rep)), device_id_type=MESH
        )
        return carry

    lax.fori_loop(1, total, greet, 0)

    loads = [
        pltpu.make_async_copy(occ_in, occ_ref, load_sem.at[0]),
        pltpu.make_async_copy(vir_in, vir_ref, load_sem.at[1]),
        pltpu.make_async_copy(count_in, count_ref, load_sem.at[2]),
        pltpu.make_async_copy(width_in, width_ref, load_sem.at[3]),
    ]
    own_load = pltpu.make_async_copy(v_ref, v_all.at[rep], v_load)
    for load in loads:
        load.start()
    own_load.start()
    for load in loads:
        load.wait()

    lane = lax.broadcasted_iota(jnp.int32, (sub, row_count), 1)
    sublane = lax.broadcasted_iota(jnp.int32, (sub, row_count), 0)
    pick = lane == sublane + rep * sub
    for group in range(n_wide):
        row = jnp.broadcast_to(occ_ref[group:group + 1, :], (sub, row_count))
        column = jnp.sum(jnp.where(pick, row, 0.0), axis=1, keepdims=True)
        e_src[group] = jnp.broadcast_to(column, (sub, 128))
    vir_src[...] = jnp.broadcast_to(vir_ref[pl.ds(wide, 1), :], vir_src.shape)

    pl.semaphore_wait(barrier, total - 1)

    chip_copies = []
    for chunk in range(chunks):
        span = pl.ds(chunk * piece, piece)
        copy = pltpu.make_async_remote_copy(
            src_ref=v_ref.at[span], dst_ref=v_all.at[rep, span],
            send_sem=chip_send.at[chunk], recv_sem=chip_recv.at[chunk],
            device_id=(wide, mirror), device_id_type=MESH,
        )
        copy.start()
        chip_copies.append(copy)
    pair_copy = pltpu.make_async_remote_copy(
        src_ref=v_ref, dst_ref=v_all.at[rep], send_sem=pair_send, recv_sem=pair_recv,
        device_id=(wide, pair), device_id_type=MESH,
    )
    pair_copy.start()

    def send_driver(step, carry):
        other = lax.rem(me + step, total)
        group = lax.div(other, n_rep)
        share = lax.rem(other, n_rep)
        pltpu.make_async_remote_copy(
            src_ref=d_ref.at[pl.ds(pl.multiple_of(group * row_count + share * sub, sub), sub)],
            dst_ref=d_all.at[rep, pl.ds(pl.multiple_of(wide * sub, sub), sub)],
            send_sem=d_send, recv_sem=d_recv,
            device_id=(group, share), device_id_type=MESH,
        ).start()
        return carry

    lax.fori_loop(1, total, send_driver, 0)
    pltpu.make_async_copy(
        d_ref.at[pl.ds(pl.multiple_of(wide * row_count + rep * sub, sub), sub)],
        d_all.at[rep, pl.ds(pl.multiple_of(wide * sub, sub), sub)],
        d_recv,
    ).start()
    for step in range(1, n_rep):
        pltpu.make_async_remote_copy(
            src_ref=vir_src, dst_ref=vir_all.at[rep], send_sem=vir_send, recv_sem=vir_recv,
            device_id=(wide, lax.rem(rep + step, n_rep)), device_id_type=MESH,
        ).start()
    pltpu.make_async_copy(vir_src, vir_all.at[rep], vir_recv).start()
    for step in range(1, n_wide):
        group = lax.rem(wide + step, n_wide)
        pltpu.make_async_remote_copy(
            src_ref=e_src.at[group], dst_ref=e_all.at[wide], send_sem=e_send, recv_sem=e_recv,
            device_id=(group, rep), device_id_type=MESH,
        ).start()
    pltpu.make_async_copy(e_src.at[wide], e_all.at[wide], e_recv).start()

    def hold(block, value):
        high, low = split(value)
        v_high[block] = high
        v_low[block] = low

    own_load.wait()
    hold(rep, v_all[rep])
    pair_copy.wait_recv()
    hold(pair, v_all[pair])

    pltpu.make_async_copy(e_all, e_all, e_recv).wait()
    pltpu.make_async_copy(vir_all, vir_all, vir_recv).wait()
    pltpu.make_async_copy(d_all, d_all, d_recv).wait()

    count = count_ref[wide]
    live_width = width_ref[wide]
    local = lax.broadcasted_iota(jnp.int32, (rows, 128), 0)
    row_id = lax.div(local, sub) * row_count + rep * sub + lax.rem(local, sub)
    col_id = lax.broadcasted_iota(jnp.int32, (rows, 128), 1)
    occ = e_all[...].reshape(rows, 128)
    weighting = []
    for block in range(n_rep):
        live = ((row_id < count) & (col_id + block * depth < live_width)).astype(F32)
        vir = jnp.broadcast_to(vir_all[block, 0:1, :], (rows, 128))
        weighting.append(live / (vir - occ))
    driver = [d_all[block] for block in range(n_rep)]
    for block in range(n_rep):
        high, low = split(driver[block] * weighting[block])
        a_high[block] = high
        a_low[block] = low

    def half_product(which):
        first = 2 * which
        return product(
            jnp.concatenate([a_high[first], a_high[first + 1]], axis=1),
            jnp.concatenate([a_low[first], a_low[first + 1]], axis=1),
            v_high[pl.ds(first, 2)].reshape(2 * depth, width),
            v_low[pl.ds(first, 2)].reshape(2 * depth, width),
        )

    ladder = half_product(half)

    relays = []
    for chunk in range(chunks):
        span = pl.ds(chunk * piece, piece)
        chip_copies[chunk].wait_recv()
        relay = pltpu.make_async_remote_copy(
            src_ref=v_all.at[mirror, span], dst_ref=v_all.at[mirror, span],
            send_sem=relay_send.at[chunk], recv_sem=relay_recv.at[chunk],
            device_id=(wide, pair), device_id_type=MESH,
        )
        relay.start()
        relays.append(relay)
    hold(mirror, v_all[mirror])
    for relay in relays:
        relay.wait_recv()
    far = lax.rem(pair + 2, n_rep)
    hold(far, v_all[far])
    ladder = ladder + half_product(1 - half)

    for sweep in range(1, ITERS):
        for block in range(n_rep):
            part = ladder[:, block * depth:(block + 1) * depth]
            high, low = split((driver[block] + part) * weighting[block])
            a_high[block] = high
            a_low[block] = low
        ladder = half_product(0) + half_product(1)
    for block in range(n_rep):
        part = ladder[:, block * depth:(block + 1) * depth]
        stage[block] = (driver[block] + part) * weighting[block]

    def send_out(step, carry):
        other = lax.rem(me + step, total)
        owner = lax.div(other, n_rep)
        block = lax.rem(other, n_rep)
        pltpu.make_async_remote_copy(
            src_ref=stage.at[block, pl.ds(pl.multiple_of(owner * sub, sub), sub)],
            dst_ref=out_ref.at[pl.ds(pl.multiple_of(wide * row_count + rep * sub, sub), sub)],
            send_sem=out_send, recv_sem=out_recv,
            device_id=(owner, block), device_id_type=MESH,
        ).start()
        return carry

    lax.fori_loop(1, total, send_out, 0)
    pltpu.make_async_copy(
        stage.at[rep, pl.ds(pl.multiple_of(wide * sub, sub), sub)],
        out_ref.at[pl.ds(pl.multiple_of(wide * row_count + rep * sub, sub), sub)],
        out_recv,
    ).start()

    for copy in chip_copies:
        copy.wait_send()
    pair_copy.wait_send()
    for relay in relays:
        relay.wait_send()
    sent = d_ref.at[pl.ds(0, (total - 1) * sub)]
    pltpu.make_async_copy(sent, sent, d_send).wait()
    sent = e_src.at[pl.ds(0, n_wide - 1)]
    pltpu.make_async_copy(sent, sent, e_send).wait()
    sent = vir_all.at[pl.ds(0, n_rep - 1)]
    pltpu.make_async_copy(sent, sent, vir_send).wait()
    sent = d_ref.at[pl.ds(0, (total - 1) * sub)]
    pltpu.make_async_copy(sent, sent, out_send).wait()
    pltpu.make_async_copy(out_ref, out_ref, out_recv).wait()


def group_shards(integrals, driver, occ_energy, vir_energy, occ_count, tile_width):
    n_wide = lax.axis_size("wide")
    n_rep = lax.axis_size("rep")
    groups, row_count, _, depth = driver.shape
    width = integrals.shape[3]
    sub = row_count // n_rep
    rows = n_wide * sub
    chunks = 4
    vmem = pl.BlockSpec(memory_space=pltpu.VMEM)
    dma = pltpu.SemaphoreType.DMA
    out = pl.pallas_call(
        functools.partial(ladder_kernel, n_wide, n_rep, chunks),
        out_shape=pltpu.VMEM((groups * row_count, depth), F32),
        in_specs=[pl.BlockSpec(memory_space=pltpu.HBM)] * 6,
        out_specs=vmem,
        scratch_shapes=[
            pltpu.SMEM((groups,), jnp.int32),
            pltpu.SMEM((groups,), jnp.int32),
            pltpu.VMEM(occ_energy.shape, F32),
            pltpu.VMEM((groups, depth), F32),
            dma((4,)), dma,
            pltpu.VMEM((n_rep, depth, width), F32),
            pltpu.VMEM((n_rep, depth, width), BF16),
            pltpu.VMEM((n_rep, depth, width), BF16),
            pltpu.VMEM((n_rep, rows, depth), F32),
            pltpu.VMEM((n_rep, rows, depth), BF16),
            pltpu.VMEM((n_rep, rows, depth), BF16),
            pltpu.VMEM((n_wide, sub, 128), F32),
            pltpu.VMEM((n_wide, sub, 128), F32),
            pltpu.VMEM((8, 128), F32),
            pltpu.VMEM((n_rep, 8, 128), F32),
            pltpu.VMEM((n_rep, rows, depth), F32),
            dma((chunks,)), dma((chunks,)), dma, dma, dma((chunks,)), dma((chunks,)),
            dma, dma, dma, dma, dma, dma, dma, dma,
        ],
        compiler_params=pltpu.CompilerParams(
            collective_id=0, has_side_effects=True, vmem_limit_bytes=60 * 1024 * 1024
        ),
        name="ladder_sweeps",
    )(
        occ_count,
        tile_width.reshape(groups),
        integrals.reshape(depth, width),
        driver.reshape(groups * row_count, depth),
        occ_energy,
        vir_energy.reshape(groups, depth),
    )
    return out.reshape(groups, row_count, 1, depth)


def tiled_shards(integrals, driver, occ_energy, vir_energy, occ_count, tile_width):
    n_wide = lax.axis_size("wide")
    wide_index = lax.axis_index("wide")
    rep_index = lax.axis_index("rep")
    groups = driver.shape[0]
    row_count = driver.shape[1]
    tile_count = driver.shape[2]
    quarter = driver.shape[3]
    out_width = integrals.shape[3]
    all_rows = row_count * n_wide
    row_ids = wide_index * row_count + jnp.arange(row_count, dtype=jnp.int32)
    col_ids = rep_index * quarter + jnp.arange(quarter, dtype=jnp.int32)
    rows_live = row_ids[None, :] < occ_count[:, None]
    cols_live = col_ids[None, None, :] < tile_width[:, :, None]
    live_mask = (rows_live[:, :, None, None] & cols_live[:, None, :, :]).astype(jnp.float32)
    weighting = live_mask / (vir_energy[:, None, :, :] - occ_energy[:, :, None, None])
    amplitudes = driver * weighting
    weights = integrals.reshape(tile_count * quarter, out_width)
    for sweep in range(ITERS):

        def add_tile(tile_index, running):
            tile_piece = lax.dynamic_index_in_dim(amplitudes, tile_index, 2, keepdims=False)
            outgoing = jnp.broadcast_to(
                tile_piece[:, None], (groups, n_wide // groups, row_count, quarter)
            )
            outgoing = outgoing.reshape(n_wide, row_count, quarter)
            received = lax.all_to_all(outgoing, "wide", split_axis=0, concat_axis=1, tiled=True)
            tile_rows = received.reshape(all_rows, quarter)
            tile_slice = lax.dynamic_slice_in_dim(weights, tile_index * quarter, quarter, 0)
            return running + jnp.dot(
                tile_rows,
                tile_slice,
                precision=lax.Precision.HIGHEST,
                preferred_element_type=jnp.float32,
            )

        partial_value = lax.fori_loop(
            0, tile_count, add_tile, jnp.zeros((all_rows, out_width), jnp.float32)
        )
        reduced = lax.psum_scatter(partial_value, "rep", scatter_dimension=1, tiled=True)
        returned = lax.all_to_all(
            reduced.reshape(1, all_rows, quarter),
            "wide",
            split_axis=1,
            concat_axis=0,
            tiled=True,
        )
        returned = returned.reshape(groups, tile_count, row_count, quarter)
        amplitudes = (driver + jnp.transpose(returned, (0, 2, 1, 3))) * weighting
    return amplitudes


def shards(integrals, driver, occ_energy, vir_energy, occ_count, tile_width):
    n_wide = lax.axis_size("wide")
    n_rep = lax.axis_size("rep")
    groups, row_count, tile_count, depth = driver.shape
    fits = tile_count == 1 and groups == n_wide and n_rep == 4 and row_count == 8 * n_rep and depth == 128
    body = group_shards if fits else tiled_shards
    return body(integrals, driver, occ_energy, vir_energy, occ_count, tile_width)


def solution(mesh):
    placed = (
        P("wide", None, "rep", None),
        P(None, "wide", None, "rep"),
        P(None, "wide"),
        P(None, None, "rep"),
        P(),
        P(),
    )
    return jax.shard_map(
        shards, mesh=mesh, in_specs=placed, out_specs=P(None, "wide", None, "rep"), check_vma=False
    )
```

```python
import functools

import jax
import jax.numpy as jnp
from jax import lax
from jax.experimental import pallas as pl
from jax.experimental.pallas import tpu as pltpu
from jax.sharding import PartitionSpec as P

ITERS = 2
PLANE = 2
MESH = pl.DeviceIdType.MESH
F32 = jnp.float32
BF16 = jnp.bfloat16


def split(value):
    high = value.astype(BF16)
    low = (value - high.astype(F32)).astype(BF16)
    return high, low


def product(high, low, weight_high, weight_low):
    dot = functools.partial(jnp.dot, preferred_element_type=F32)
    return dot(high, weight_high) + (dot(low, weight_high) + dot(high, weight_low))


def ladder_kernel(
    n_wide, n_rep, chunks,
    count_in, width_in, v_ref, d_ref, occ_in, vir_in, out_ref,
    count_ref, width_ref, occ_ref, vir_ref, load_sem, v_load, v_all, v_high, v_low, d_all, a_high, a_low, e_src, e_all, vir_src, vir_all, stage,
    up_sem, down_sem, chip_send, chip_recv, pair_send, pair_recv, relay_send, relay_recv,
    d_send, d_recv, e_send, e_recv, vir_send, vir_recv, out_send, out_recv,
):
    wide = lax.axis_index("wide")
    rep = lax.axis_index("rep")
    total = n_wide * n_rep
    me = wide * n_rep + rep
    depth, width = v_ref.shape
    sub = 8
    row_count = sub * n_rep
    rows = n_wide * sub
    half = lax.div(rep, 2)
    pair = rep + 1 - 2 * lax.rem(rep, 2)
    mirror = lax.rem(rep + 2, n_rep)
    piece = depth // chunks

    barrier = pltpu.get_barrier_semaphore()

    plane = lax.div(wide, PLANE)
    planes = n_wide // PLANE
    mates = PLANE * n_rep
    place = me - plane * mates
    above = (lax.min(wide + PLANE, n_wide - 1), rep)
    below = (lax.max(wide - PLANE, 0), rep)

    def tell(semaphore, device):
        pl.semaphore_signal(semaphore, inc=1, device_id=device, device_id_type=MESH)

    for step in range(1, mates):
        other = plane * mates + lax.rem(place + step, mates)
        tell(barrier, (lax.div(other, n_rep), lax.rem(other, n_rep)))

    @pl.when(plane < planes - 1)
    def _():
        tell(barrier, above)

    @pl.when(plane > 0)
    def _():
        tell(barrier, below)

    loads = [
        pltpu.make_async_copy(occ_in, occ_ref, load_sem.at[0]),
        pltpu.make_async_copy(vir_in, vir_ref, load_sem.at[1]),
        pltpu.make_async_copy(count_in, count_ref, load_sem.at[2]),
        pltpu.make_async_copy(width_in, width_ref, load_sem.at[3]),
    ]
    own_load = pltpu.make_async_copy(v_ref, v_all.at[rep], v_load)
    for load in loads:
        load.start()
    own_load.start()
    for load in loads:
        load.wait()

    lane = lax.broadcasted_iota(jnp.int32, (sub, row_count), 1)
    sublane = lax.broadcasted_iota(jnp.int32, (sub, row_count), 0)
    pick = lane == sublane + rep * sub
    for group in range(n_wide):
        row = jnp.broadcast_to(occ_ref[group:group + 1, :], (sub, row_count))
        column = jnp.sum(jnp.where(pick, row, 0.0), axis=1, keepdims=True)
        e_src[group] = jnp.broadcast_to(column, (sub, 128))
    vir_src[...] = jnp.broadcast_to(vir_ref[pl.ds(wide, 1), :], vir_src.shape)

    beside = jnp.where(plane > 0, 1, 0) + jnp.where(plane < planes - 1, 1, 0)
    pl.semaphore_wait(barrier, mates - 1 + beside)

    chip_copies = []
    for chunk in range(chunks):
        span = pl.ds(chunk * piece, piece)
        copy = pltpu.make_async_remote_copy(
            src_ref=v_ref.at[span], dst_ref=v_all.at[rep, span],
            send_sem=chip_send.at[chunk], recv_sem=chip_recv.at[chunk],
            device_id=(wide, mirror), device_id_type=MESH,
        )
        copy.start()
        chip_copies.append(copy)
    pair_copy = pltpu.make_async_remote_copy(
        src_ref=v_ref, dst_ref=v_all.at[rep], send_sem=pair_send, recv_sem=pair_recv,
        device_id=(wide, pair), device_id_type=MESH,
    )
    pair_copy.start()

    @pl.when(plane > 0)
    def _():
        pl.semaphore_wait(up_sem, 1)

    @pl.when(plane < planes - 1)
    def _():
        tell(up_sem, above)
        pl.semaphore_wait(down_sem, 1)

    @pl.when(plane > 0)
    def _():
        tell(down_sem, below)

    def send_driver(step, carry):
        other = lax.rem(me + step, total)
        group = lax.div(other, n_rep)
        share = lax.rem(other, n_rep)
        pltpu.make_async_remote_copy(
            src_ref=d_ref.at[pl.ds(pl.multiple_of(group * row_count + share * sub, sub), sub)],
            dst_ref=d_all.at[rep, pl.ds(pl.multiple_of(wide * sub, sub), sub)],
            send_sem=d_send, recv_sem=d_recv,
            device_id=(group, share), device_id_type=MESH,
        ).start()
        return carry

    lax.fori_loop(1, total, send_driver, 0)
    pltpu.make_async_copy(
        d_ref.at[pl.ds(pl.multiple_of(wide * row_count + rep * sub, sub), sub)],
        d_all.at[rep, pl.ds(pl.multiple_of(wide * sub, sub), sub)],
        d_recv,
    ).start()
    for step in range(1, n_rep):
        pltpu.make_async_remote_copy(
            src_ref=vir_src, dst_ref=vir_all.at[rep], send_sem=vir_send, recv_sem=vir_recv,
            device_id=(wide, lax.rem(rep + step, n_rep)), device_id_type=MESH,
        ).start()
    pltpu.make_async_copy(vir_src, vir_all.at[rep], vir_recv).start()
    for step in range(1, n_wide):
        group = lax.rem(wide + step, n_wide)
        pltpu.make_async_remote_copy(
            src_ref=e_src.at[group], dst_ref=e_all.at[wide], send_sem=e_send, recv_sem=e_recv,
            device_id=(group, rep), device_id_type=MESH,
        ).start()
    pltpu.make_async_copy(e_src.at[wide], e_all.at[wide], e_recv).start()

    def hold(block, value):
        high, low = split(value)
        v_high[block] = high
        v_low[block] = low

    own_load.wait()
    hold(rep, v_all[rep])
    pair_copy.wait_recv()
    hold(pair, v_all[pair])

    pltpu.make_async_copy(e_all, e_all, e_recv).wait()
    pltpu.make_async_copy(vir_all, vir_all, vir_recv).wait()
    pltpu.make_async_copy(d_all, d_all, d_recv).wait()

    count = count_ref[wide]
    live_width = width_ref[wide]
    local = lax.broadcasted_iota(jnp.int32, (rows, 128), 0)
    row_id = lax.div(local, sub) * row_count + rep * sub + lax.rem(local, sub)
    col_id = lax.broadcasted_iota(jnp.int32, (rows, 128), 1)
    occ = e_all[...].reshape(rows, 128)
    weighting = []
    for block in range(n_rep):
        live = ((row_id < count) & (col_id + block * depth < live_width)).astype(F32)
        vir = jnp.broadcast_to(vir_all[block, 0:1, :], (rows, 128))
        weighting.append(live / (vir - occ))
    driver = [d_all[block] for block in range(n_rep)]
    for block in range(n_rep):
        high, low = split(driver[block] * weighting[block])
        a_high[block] = high
        a_low[block] = low

    def half_product(which):
        first = 2 * which
        return product(
            jnp.concatenate([a_high[first], a_high[first + 1]], axis=1),
            jnp.concatenate([a_low[first], a_low[first + 1]], axis=1),
            v_high[pl.ds(first, 2)].reshape(2 * depth, width),
            v_low[pl.ds(first, 2)].reshape(2 * depth, width),
        )

    ladder = half_product(half)

    relays = []
    for chunk in range(chunks):
        span = pl.ds(chunk * piece, piece)
        chip_copies[chunk].wait_recv()
        relay = pltpu.make_async_remote_copy(
            src_ref=v_all.at[mirror, span], dst_ref=v_all.at[mirror, span],
            send_sem=relay_send.at[chunk], recv_sem=relay_recv.at[chunk],
            device_id=(wide, pair), device_id_type=MESH,
        )
        relay.start()
        relays.append(relay)
    hold(mirror, v_all[mirror])
    for relay in relays:
        relay.wait_recv()
    far = lax.rem(pair + 2, n_rep)
    hold(far, v_all[far])
    ladder = ladder + half_product(1 - half)

    for sweep in range(1, ITERS):
        for block in range(n_rep):
            part = ladder[:, block * depth:(block + 1) * depth]
            high, low = split((driver[block] + part) * weighting[block])
            a_high[block] = high
            a_low[block] = low
        ladder = half_product(0) + half_product(1)
    for block in range(n_rep):
        part = ladder[:, block * depth:(block + 1) * depth]
        stage[block] = (driver[block] + part) * weighting[block]

    def send_out(step, carry):
        other = lax.rem(me + step, total)
        owner = lax.div(other, n_rep)
        block = lax.rem(other, n_rep)
        pltpu.make_async_remote_copy(
            src_ref=stage.at[block, pl.ds(pl.multiple_of(owner * sub, sub), sub)],
            dst_ref=out_ref.at[pl.ds(pl.multiple_of(wide * row_count + rep * sub, sub), sub)],
            send_sem=out_send, recv_sem=out_recv,
            device_id=(owner, block), device_id_type=MESH,
        ).start()
        return carry

    lax.fori_loop(1, total, send_out, 0)
    pltpu.make_async_copy(
        stage.at[rep, pl.ds(pl.multiple_of(wide * sub, sub), sub)],
        out_ref.at[pl.ds(pl.multiple_of(wide * row_count + rep * sub, sub), sub)],
        out_recv,
    ).start()

    for copy in chip_copies:
        copy.wait_send()
    pair_copy.wait_send()
    for relay in relays:
        relay.wait_send()
    sent = d_ref.at[pl.ds(0, (total - 1) * sub)]
    pltpu.make_async_copy(sent, sent, d_send).wait()
    sent = e_src.at[pl.ds(0, n_wide - 1)]
    pltpu.make_async_copy(sent, sent, e_send).wait()
    sent = vir_all.at[pl.ds(0, n_rep - 1)]
    pltpu.make_async_copy(sent, sent, vir_send).wait()
    sent = d_ref.at[pl.ds(0, (total - 1) * sub)]
    pltpu.make_async_copy(sent, sent, out_send).wait()
    pltpu.make_async_copy(out_ref, out_ref, out_recv).wait()


def group_shards(integrals, driver, occ_energy, vir_energy, occ_count, tile_width):
    n_wide = lax.axis_size("wide")
    n_rep = lax.axis_size("rep")
    groups, row_count, _, depth = driver.shape
    width = integrals.shape[3]
    sub = row_count // n_rep
    rows = n_wide * sub
    chunks = 4
    vmem = pl.BlockSpec(memory_space=pltpu.VMEM)
    dma = pltpu.SemaphoreType.DMA
    out = pl.pallas_call(
        functools.partial(ladder_kernel, n_wide, n_rep, chunks),
        out_shape=pltpu.VMEM((groups * row_count, depth), F32),
        in_specs=[pl.BlockSpec(memory_space=pltpu.HBM)] * 6,
        out_specs=vmem,
        scratch_shapes=[
            pltpu.SMEM((groups,), jnp.int32),
            pltpu.SMEM((groups,), jnp.int32),
            pltpu.VMEM(occ_energy.shape, F32),
            pltpu.VMEM((groups, depth), F32),
            dma((4,)), dma,
            pltpu.VMEM((n_rep, depth, width), F32),
            pltpu.VMEM((n_rep, depth, width), BF16),
            pltpu.VMEM((n_rep, depth, width), BF16),
            pltpu.VMEM((n_rep, rows, depth), F32),
            pltpu.VMEM((n_rep, rows, depth), BF16),
            pltpu.VMEM((n_rep, rows, depth), BF16),
            pltpu.VMEM((n_wide, sub, 128), F32),
            pltpu.VMEM((n_wide, sub, 128), F32),
            pltpu.VMEM((8, 128), F32),
            pltpu.VMEM((n_rep, 8, 128), F32),
            pltpu.VMEM((n_rep, rows, depth), F32),
            pltpu.SemaphoreType.REGULAR, pltpu.SemaphoreType.REGULAR,
            dma((chunks,)), dma((chunks,)), dma, dma, dma((chunks,)), dma((chunks,)),
            dma, dma, dma, dma, dma, dma, dma, dma,
        ],
        compiler_params=pltpu.CompilerParams(
            collective_id=0, has_side_effects=True, vmem_limit_bytes=60 * 1024 * 1024
        ),
        name="ladder_sweeps",
    )(
        occ_count,
        tile_width.reshape(groups),
        integrals.reshape(depth, width),
        driver.reshape(groups * row_count, depth),
        occ_energy,
        vir_energy.reshape(groups, depth),
    )
    return out.reshape(groups, row_count, 1, depth)


def tiled_shards(integrals, driver, occ_energy, vir_energy, occ_count, tile_width):
    n_wide = lax.axis_size("wide")
    wide_index = lax.axis_index("wide")
    rep_index = lax.axis_index("rep")
    groups = driver.shape[0]
    row_count = driver.shape[1]
    tile_count = driver.shape[2]
    quarter = driver.shape[3]
    out_width = integrals.shape[3]
    all_rows = row_count * n_wide
    row_ids = wide_index * row_count + jnp.arange(row_count, dtype=jnp.int32)
    col_ids = rep_index * quarter + jnp.arange(quarter, dtype=jnp.int32)
    rows_live = row_ids[None, :] < occ_count[:, None]
    cols_live = col_ids[None, None, :] < tile_width[:, :, None]
    live_mask = (rows_live[:, :, None, None] & cols_live[:, None, :, :]).astype(jnp.float32)
    weighting = live_mask / (vir_energy[:, None, :, :] - occ_energy[:, :, None, None])
    amplitudes = driver * weighting
    weights = integrals.reshape(tile_count * quarter, out_width)
    for sweep in range(ITERS):

        def add_tile(tile_index, running):
            tile_piece = lax.dynamic_index_in_dim(amplitudes, tile_index, 2, keepdims=False)
            outgoing = jnp.broadcast_to(
                tile_piece[:, None], (groups, n_wide // groups, row_count, quarter)
            )
            outgoing = outgoing.reshape(n_wide, row_count, quarter)
            received = lax.all_to_all(outgoing, "wide", split_axis=0, concat_axis=1, tiled=True)
            tile_rows = received.reshape(all_rows, quarter)
            tile_slice = lax.dynamic_slice_in_dim(weights, tile_index * quarter, quarter, 0)
            return running + jnp.dot(
                tile_rows,
                tile_slice,
                precision=lax.Precision.HIGHEST,
                preferred_element_type=jnp.float32,
            )

        partial_value = lax.fori_loop(
            0, tile_count, add_tile, jnp.zeros((all_rows, out_width), jnp.float32)
        )
        reduced = lax.psum_scatter(partial_value, "rep", scatter_dimension=1, tiled=True)
        returned = lax.all_to_all(
            reduced.reshape(1, all_rows, quarter),
            "wide",
            split_axis=1,
            concat_axis=0,
            tiled=True,
        )
        returned = returned.reshape(groups, tile_count, row_count, quarter)
        amplitudes = (driver + jnp.transpose(returned, (0, 2, 1, 3))) * weighting
    return amplitudes


def shards(integrals, driver, occ_energy, vir_energy, occ_count, tile_width):
    n_wide = lax.axis_size("wide")
    n_rep = lax.axis_size("rep")
    groups, row_count, tile_count, depth = driver.shape
    fits = tile_count == 1 and groups == n_wide and n_wide % PLANE == 0 and n_rep == 4 and row_count == 8 * n_rep and depth == 128
    body = group_shards if fits else tiled_shards
    return body(integrals, driver, occ_energy, vir_energy, occ_count, tile_width)


def solution(mesh):
    placed = (
        P("wide", None, "rep", None),
        P(None, "wide", None, "rep"),
        P(None, "wide"),
        P(None, None, "rep"),
        P(),
        P(),
    )
    return jax.shard_map(
        shards, mesh=mesh, in_specs=placed, out_specs=P(None, "wide", None, "rep"), check_vma=False
    )
```

```python
import functools

import jax
import jax.numpy as jnp
from jax import lax
from jax.experimental import pallas as pl
from jax.experimental.pallas import tpu as pltpu
from jax.sharding import PartitionSpec as P

ITERS = 2
PLANE = 2
MESH = pl.DeviceIdType.MESH
F32 = jnp.float32
BF16 = jnp.bfloat16


def split(value):
    high = value.astype(BF16)
    low = (value - high.astype(F32)).astype(BF16)
    return high, low


def product(high, low, weight_high, weight_low):
    dot = functools.partial(jnp.dot, preferred_element_type=F32)
    return dot(high, weight_high) + (dot(low, weight_high) + dot(high, weight_low))


def ladder_kernel(
    n_wide, n_rep, chunks,
    count_in, width_in, v_ref, d_ref, occ_in, vir_in, out_ref,
    count_ref, width_ref, occ_ref, vir_ref, load_sem, v_load, v_all, v_high, v_low, d_all, a_high, a_low, e_src, e_all, vir_src, vir_all, stage,
    up_sem, down_sem, chip_send, chip_recv, pair_send, pair_recv, relay_send, relay_recv,
    d_send, d_recv, e_send, e_recv, vir_send, vir_recv, out_send, out_recv,
):
    wide = lax.axis_index("wide")
    rep = lax.axis_index("rep")
    total = n_wide * n_rep
    me = wide * n_rep + rep
    depth, width = v_ref.shape
    sub = 8
    row_count = sub * n_rep
    rows = n_wide * sub
    half = lax.div(rep, 2)
    pair = rep + 1 - 2 * lax.rem(rep, 2)
    mirror = lax.rem(rep + 2, n_rep)
    piece = depth // chunks

    barrier = pltpu.get_barrier_semaphore()

    plane = lax.div(wide, PLANE)
    planes = n_wide // PLANE
    mates = PLANE * n_rep
    place = me - plane * mates
    above = (lax.min(wide + PLANE, n_wide - 1), rep)
    below = (lax.max(wide - PLANE, 0), rep)

    def tell(semaphore, device):
        pl.semaphore_signal(semaphore, inc=1, device_id=device, device_id_type=MESH)

    for step in range(1, mates):
        other = plane * mates + lax.rem(place + step, mates)
        tell(barrier, (lax.div(other, n_rep), lax.rem(other, n_rep)))

    @pl.when(plane < planes - 1)
    def _():
        tell(barrier, above)

    @pl.when(plane > 0)
    def _():
        tell(barrier, below)

    loads = [
        pltpu.make_async_copy(occ_in, occ_ref, load_sem.at[0]),
        pltpu.make_async_copy(vir_in, vir_ref, load_sem.at[1]),
        pltpu.make_async_copy(count_in, count_ref, load_sem.at[2]),
        pltpu.make_async_copy(width_in, width_ref, load_sem.at[3]),
    ]
    own_load = pltpu.make_async_copy(v_ref, v_all.at[rep], v_load)
    for load in loads:
        load.start()
    own_load.start()
    for load in loads:
        load.wait()

    lane = lax.broadcasted_iota(jnp.int32, (sub, row_count), 1)
    sublane = lax.broadcasted_iota(jnp.int32, (sub, row_count), 0)
    pick = lane == sublane + rep * sub
    for group in range(n_wide):
        row = jnp.broadcast_to(occ_ref[group:group + 1, :], (sub, row_count))
        column = jnp.sum(jnp.where(pick, row, 0.0), axis=1, keepdims=True)
        e_src[group] = jnp.broadcast_to(column, (sub, 128))
    vir_src[...] = jnp.broadcast_to(vir_ref[pl.ds(wide, 1), :], vir_src.shape)

    beside = jnp.where(plane > 0, 1, 0) + jnp.where(plane < planes - 1, 1, 0)
    pl.semaphore_wait(barrier, mates - 1 + beside)

    chip_copies = []
    for chunk in range(chunks):
        span = pl.ds(chunk * piece, piece)
        copy = pltpu.make_async_remote_copy(
            src_ref=v_ref.at[span], dst_ref=v_all.at[rep, span],
            send_sem=chip_send.at[chunk], recv_sem=chip_recv.at[chunk],
            device_id=(wide, mirror), device_id_type=MESH,
        )
        copy.start()
        chip_copies.append(copy)
    pair_copy = pltpu.make_async_remote_copy(
        src_ref=v_ref, dst_ref=v_all.at[rep], send_sem=pair_send, recv_sem=pair_recv,
        device_id=(wide, pair), device_id_type=MESH,
    )
    pair_copy.start()

    @pl.when(plane > 0)
    def _():
        pl.semaphore_wait(up_sem, 1)

    @pl.when(plane < planes - 1)
    def _():
        tell(up_sem, above)
        pl.semaphore_wait(down_sem, 1)

    @pl.when(plane > 0)
    def _():
        tell(down_sem, below)

    def send_driver(step, carry):
        other = lax.rem(me + step, total)
        group = lax.div(other, n_rep)
        share = lax.rem(other, n_rep)
        pltpu.make_async_remote_copy(
            src_ref=d_ref.at[pl.ds(pl.multiple_of(group * row_count + share * sub, sub), sub)],
            dst_ref=d_all.at[rep, pl.ds(pl.multiple_of(wide * sub, sub), sub)],
            send_sem=d_send, recv_sem=d_recv,
            device_id=(group, share), device_id_type=MESH,
        ).start()
        return carry

    lax.fori_loop(1, total, send_driver, 0)
    pltpu.make_async_copy(
        d_ref.at[pl.ds(pl.multiple_of(wide * row_count + rep * sub, sub), sub)],
        d_all.at[rep, pl.ds(pl.multiple_of(wide * sub, sub), sub)],
        d_recv,
    ).start()
    for step in range(1, n_rep):
        pltpu.make_async_remote_copy(
            src_ref=vir_src, dst_ref=vir_all.at[rep], send_sem=vir_send, recv_sem=vir_recv,
            device_id=(wide, lax.rem(rep + step, n_rep)), device_id_type=MESH,
        ).start()
    pltpu.make_async_copy(vir_src, vir_all.at[rep], vir_recv).start()
    for step in range(1, n_wide):
        group = lax.rem(wide + step, n_wide)
        pltpu.make_async_remote_copy(
            src_ref=e_src.at[group], dst_ref=e_all.at[wide], send_sem=e_send, recv_sem=e_recv,
            device_id=(group, rep), device_id_type=MESH,
        ).start()
    pltpu.make_async_copy(e_src.at[wide], e_all.at[wide], e_recv).start()

    def hold(block, value):
        high, low = split(value)
        v_high[block] = high
        v_low[block] = low

    own_load.wait()
    hold(rep, v_all[rep])
    pair_copy.wait_recv()
    hold(pair, v_all[pair])

    pltpu.make_async_copy(e_all, e_all, e_recv).wait()
    pltpu.make_async_copy(vir_all, vir_all, vir_recv).wait()
    pltpu.make_async_copy(d_all, d_all, d_recv).wait()

    count = count_ref[wide]
    live_width = width_ref[wide]
    local = lax.broadcasted_iota(jnp.int32, (rows, 128), 0)
    row_id = lax.div(local, sub) * row_count + rep * sub + lax.rem(local, sub)
    col_id = lax.broadcasted_iota(jnp.int32, (rows, 128), 1)
    occ = e_all[...].reshape(rows, 128)
    weighting = []
    for block in range(n_rep):
        live = ((row_id < count) & (col_id + block * depth < live_width)).astype(F32)
        vir = jnp.broadcast_to(vir_all[block, 0:1, :], (rows, 128))
        weighting.append(live / (vir - occ))
    driver = [d_all[block] for block in range(n_rep)]
    for block in range(n_rep):
        high, low = split(driver[block] * weighting[block])
        a_high[block] = high
        a_low[block] = low

    def half_product(which, columns=pl.ds(0, width)):
        first = 2 * which
        return product(
            jnp.concatenate([a_high[first], a_high[first + 1]], axis=1),
            jnp.concatenate([a_low[first], a_low[first + 1]], axis=1),
            v_high[pl.ds(first, 2), :, columns].reshape(2 * depth, columns.size),
            v_low[pl.ds(first, 2), :, columns].reshape(2 * depth, columns.size),
        )

    ladder = half_product(half)

    relays = []
    for chunk in range(chunks):
        span = pl.ds(chunk * piece, piece)
        chip_copies[chunk].wait_recv()
        relay = pltpu.make_async_remote_copy(
            src_ref=v_all.at[mirror, span], dst_ref=v_all.at[mirror, span],
            send_sem=relay_send.at[chunk], recv_sem=relay_recv.at[chunk],
            device_id=(wide, pair), device_id_type=MESH,
        )
        relay.start()
        relays.append(relay)
    hold(mirror, v_all[mirror])
    for relay in relays:
        relay.wait_recv()
    far = lax.rem(pair + 2, n_rep)
    hold(far, v_all[far])
    ladder = ladder + half_product(1 - half)

    for sweep in range(1, ITERS):
        for block in range(n_rep):
            part = ladder[:, block * depth:(block + 1) * depth]
            high, low = split((driver[block] + part) * weighting[block])
            a_high[block] = high
            a_low[block] = low
        if sweep < ITERS - 1:
            ladder = half_product(0) + half_product(1)

    for side in range(2):
        columns = pl.ds(side * 2 * depth, 2 * depth)
        ladder = half_product(0, columns) + half_product(1, columns)
        for near in range(2):
            block = 2 * side + near
            part = ladder[:, near * depth:(near + 1) * depth]
            stage[block] = (driver[block] + part) * weighting[block]

        def send_out(turn, carry):
            owner = lax.rem(wide + 1 + lax.div(turn, 2), n_wide)
            block = 2 * side + lax.rem(turn, 2)

            @pl.when(jnp.logical_or(owner != wide, block != rep))
            def _():
                pltpu.make_async_remote_copy(
                    src_ref=stage.at[block, pl.ds(pl.multiple_of(owner * sub, sub), sub)],
                    dst_ref=out_ref.at[pl.ds(pl.multiple_of(wide * row_count + rep * sub, sub), sub)],
                    send_sem=out_send, recv_sem=out_recv,
                    device_id=(owner, block), device_id_type=MESH,
                ).start()

            return carry

        lax.fori_loop(0, 2 * n_wide, send_out, 0)
    pltpu.make_async_copy(
        stage.at[rep, pl.ds(pl.multiple_of(wide * sub, sub), sub)],
        out_ref.at[pl.ds(pl.multiple_of(wide * row_count + rep * sub, sub), sub)],
        out_recv,
    ).start()

    for copy in chip_copies:
        copy.wait_send()
    pair_copy.wait_send()
    for relay in relays:
        relay.wait_send()
    sent = d_ref.at[pl.ds(0, (total - 1) * sub)]
    pltpu.make_async_copy(sent, sent, d_send).wait()
    sent = e_src.at[pl.ds(0, n_wide - 1)]
    pltpu.make_async_copy(sent, sent, e_send).wait()
    sent = vir_all.at[pl.ds(0, n_rep - 1)]
    pltpu.make_async_copy(sent, sent, vir_send).wait()
    sent = d_ref.at[pl.ds(0, (total - 1) * sub)]
    pltpu.make_async_copy(sent, sent, out_send).wait()
    pltpu.make_async_copy(out_ref, out_ref, out_recv).wait()


def group_shards(integrals, driver, occ_energy, vir_energy, occ_count, tile_width):
    n_wide = lax.axis_size("wide")
    n_rep = lax.axis_size("rep")
    groups, row_count, _, depth = driver.shape
    width = integrals.shape[3]
    sub = row_count // n_rep
    rows = n_wide * sub
    chunks = 4
    vmem = pl.BlockSpec(memory_space=pltpu.VMEM)
    dma = pltpu.SemaphoreType.DMA
    out = pl.pallas_call(
        functools.partial(ladder_kernel, n_wide, n_rep, chunks),
        out_shape=pltpu.VMEM((groups * row_count, depth), F32),
        in_specs=[pl.BlockSpec(memory_space=pltpu.HBM)] * 6,
        out_specs=vmem,
        scratch_shapes=[
            pltpu.SMEM((groups,), jnp.int32),
            pltpu.SMEM((groups,), jnp.int32),
            pltpu.VMEM(occ_energy.shape, F32),
            pltpu.VMEM((groups, depth), F32),
            dma((4,)), dma,
            pltpu.VMEM((n_rep, depth, width), F32),
            pltpu.VMEM((n_rep, depth, width), BF16),
            pltpu.VMEM((n_rep, depth, width), BF16),
            pltpu.VMEM((n_rep, rows, depth), F32),
            pltpu.VMEM((n_rep, rows, depth), BF16),
            pltpu.VMEM((n_rep, rows, depth), BF16),
            pltpu.VMEM((n_wide, sub, 128), F32),
            pltpu.VMEM((n_wide, sub, 128), F32),
            pltpu.VMEM((8, 128), F32),
            pltpu.VMEM((n_rep, 8, 128), F32),
            pltpu.VMEM((n_rep, rows, depth), F32),
            pltpu.SemaphoreType.REGULAR, pltpu.SemaphoreType.REGULAR,
            dma((chunks,)), dma((chunks,)), dma, dma, dma((chunks,)), dma((chunks,)),
            dma, dma, dma, dma, dma, dma, dma, dma,
        ],
        compiler_params=pltpu.CompilerParams(
            collective_id=0, has_side_effects=True, vmem_limit_bytes=60 * 1024 * 1024
        ),
        name="ladder_sweeps",
    )(
        occ_count,
        tile_width.reshape(groups),
        integrals.reshape(depth, width),
        driver.reshape(groups * row_count, depth),
        occ_energy,
        vir_energy.reshape(groups, depth),
    )
    return out.reshape(groups, row_count, 1, depth)


def tiled_shards(integrals, driver, occ_energy, vir_energy, occ_count, tile_width):
    n_wide = lax.axis_size("wide")
    wide_index = lax.axis_index("wide")
    rep_index = lax.axis_index("rep")
    groups = driver.shape[0]
    row_count = driver.shape[1]
    tile_count = driver.shape[2]
    quarter = driver.shape[3]
    out_width = integrals.shape[3]
    all_rows = row_count * n_wide
    row_ids = wide_index * row_count + jnp.arange(row_count, dtype=jnp.int32)
    col_ids = rep_index * quarter + jnp.arange(quarter, dtype=jnp.int32)
    rows_live = row_ids[None, :] < occ_count[:, None]
    cols_live = col_ids[None, None, :] < tile_width[:, :, None]
    live_mask = (rows_live[:, :, None, None] & cols_live[:, None, :, :]).astype(jnp.float32)
    weighting = live_mask / (vir_energy[:, None, :, :] - occ_energy[:, :, None, None])
    amplitudes = driver * weighting
    weights = integrals.reshape(tile_count * quarter, out_width)
    for sweep in range(ITERS):

        def add_tile(tile_index, running):
            tile_piece = lax.dynamic_index_in_dim(amplitudes, tile_index, 2, keepdims=False)
            outgoing = jnp.broadcast_to(
                tile_piece[:, None], (groups, n_wide // groups, row_count, quarter)
            )
            outgoing = outgoing.reshape(n_wide, row_count, quarter)
            received = lax.all_to_all(outgoing, "wide", split_axis=0, concat_axis=1, tiled=True)
            tile_rows = received.reshape(all_rows, quarter)
            tile_slice = lax.dynamic_slice_in_dim(weights, tile_index * quarter, quarter, 0)
            return running + jnp.dot(
                tile_rows,
                tile_slice,
                precision=lax.Precision.HIGHEST,
                preferred_element_type=jnp.float32,
            )

        partial_value = lax.fori_loop(
            0, tile_count, add_tile, jnp.zeros((all_rows, out_width), jnp.float32)
        )
        reduced = lax.psum_scatter(partial_value, "rep", scatter_dimension=1, tiled=True)
        returned = lax.all_to_all(
            reduced.reshape(1, all_rows, quarter),
            "wide",
            split_axis=1,
            concat_axis=0,
            tiled=True,
        )
        returned = returned.reshape(groups, tile_count, row_count, quarter)
        amplitudes = (driver + jnp.transpose(returned, (0, 2, 1, 3))) * weighting
    return amplitudes


def shards(integrals, driver, occ_energy, vir_energy, occ_count, tile_width):
    n_wide = lax.axis_size("wide")
    n_rep = lax.axis_size("rep")
    groups, row_count, tile_count, depth = driver.shape
    fits = tile_count == 1 and groups == n_wide and n_wide % PLANE == 0 and n_rep == 4 and row_count == 8 * n_rep and depth == 128
    body = group_shards if fits else tiled_shards
    return body(integrals, driver, occ_energy, vir_energy, occ_count, tile_width)


def solution(mesh):
    placed = (
        P("wide", None, "rep", None),
        P(None, "wide", None, "rep"),
        P(None, "wide"),
        P(None, None, "rep"),
        P(),
        P(),
    )
    return jax.shard_map(
        shards, mesh=mesh, in_specs=placed, out_specs=P(None, "wide", None, "rep"), check_vma=False
    )
```
